32 devices in a mesh: gx: 2 (over y), gy: 4 (over x, core), gz: 4 (over z).
Axes of the slice: x: 2, y: 2, z: 4, core: 2. Of those that a mesh axis runs over, the one named last changes fastest.
Arguments:
- offsets: float32 [3, 4, 8, 8, 128], P(None, 'gx', 'gy', 'gz'), may hold values from -0.5 to 0.5
- lines: float32 [3, 4, 8, 8, 128], P(None, 'gx', 'gy', 'gz'), may hold values from -4 to 4
- burgers: float32 [3, 4, 8, 8, 128], P(None, 'gx', 'gy', 'gz'), may hold values from -4 to 4
- counts: int32 [4, 8, 8], P('gx', 'gy', 'gz'), may hold values from 64 to 128, as said below
- mobility: float32 [4, 8, 8], P('gx', 'gy', 'gz'), may hold values from 0.5 to 2
- stress: float32 [3, 3], replicated, may hold values from -3 to 3
- translation: float32 [128, 128], replicated, may hold values from -0.625 to 0.625
Outputs:
- velocity: float32 [3, 4, 8, 8, 128], P(None, 'gx', 'gy', 'gz')
The draws below stay inside these ranges and needn't reach their ends.
Inputs may be any that keep to these rules, and one draw needn't show every extreme that they name: `counts`: some cell holds 128 live segments.
All inputs are finite; a program needn't handle non-finite values.
Results may differ from the reference program's by a relative error of at most 0.0003.
Values sent between devices are 32-bit elements; how exact they have to be, the bound alone decides.
No kernel may reach another device: no remote copies, remote signals or barrier semaphores. Data moves between devices by JAX's collectives and lax.ppermute only.
A program may use at most 64 MiB of HBM per device.

```python
import math
import jax
import jax.numpy as jnp
from jax import lax

SLOTS = 128
TERMS = 35
EXPANSION = 128
NCX = 4
NCY = 8
NCZ = 8
CELLS = 256


def draw_counts(key, part):
    key = jax.random.fold_in(key, 7)
    primary_key, secondary_key = jax.random.split(key)
    shape = (NCX, NCY, NCZ)
    primary = jax.random.randint(primary_key, shape, 0, SLOTS)
    secondary = jax.random.randint(secondary_key, shape, 0, SLOTS)
    result = SLOTS // 2 + primary * secondary // (2 * SLOTS)
    return result.at[0, 0, 0].set(SLOTS).astype(jnp.int32)


def block_scale(own_key, shape, cuts, low, top_value):
    factor_of = 1.0
    for position, shards_of in cuts:
        heights = jax.random.uniform(jax.random.fold_in(jax.random.fold_in(own_key, 6), position), (shards_of,), jnp.float32, low / len(cuts), top_value / len(cuts))
        factor_of = factor_of * jnp.repeat(jnp.exp(heights), shape[position] // shards_of).reshape((-1,) + (1,) * (len(shape) - 1 - position))
    return factor_of


def scatter_about(own_key, dims, spread, limit, shards=(), kind=jnp.bfloat16):
    entries = spread * jax.random.normal(own_key, dims, jnp.float32)
    if shards:
        entries = entries * block_scale(own_key, dims, shards, -0.22, 0.18)
    return jnp.clip(entries, -limit, limit).astype(kind)


def setup_inputs(seed: int = 0) -> dict:
    key_list = jax.random.split(jax.random.key(seed), 8)
    return {
        "offsets": jnp.clip(jax.random.uniform(key_list[0], (3, NCX, NCY, NCZ, SLOTS), jnp.float32, -0.5, 0.5) * block_scale(key_list[0], (3, NCX, NCY, NCZ, SLOTS), ((1, 2), (2, 4), (3, 4)), -0.4, 0.0), -0.5, 0.5),
        "lines": scatter_about(key_list[1], (3, NCX, NCY, NCZ, SLOTS), 1.0, 4.0, ((1, 2), (2, 4), (3, 4)), jnp.float32),
        "burgers": scatter_about(key_list[2], (3, NCX, NCY, NCZ, SLOTS), 1.0, 4.0, ((1, 2), (2, 4), (3, 4)), jnp.float32),
        "counts": draw_counts(jax.random.fold_in(key_list[7], 71), 0),
        "mobility": jnp.clip(jnp.exp(math.log(2.0) - 1.3862944 * jax.random.uniform(key_list[4], (NCX, NCY, NCZ), jnp.float32) ** block_scale(key_list[4], (NCX, NCY, NCZ), ((0, 2), (1, 4), (2, 4)), -0.2, 0.2)), 0.5, 2.0),
        "stress": scatter_about(key_list[5], (3, 3), 0.5, 3.0, (), jnp.float32),
        "translation": scatter_about(key_list[6], (EXPANSION, EXPANSION), (3 * TERMS) ** -0.5, 0.625, (), jnp.float32),
    }


core_square = 0.0625
near_scale = 0.01
highest = lax.Precision.HIGHEST

def exponent_list():
    result = []
    for first in range(5):
        for second in range(5 - first):
            for third in range(5 - first - second):
                result.append((first, second, third))
    return result

def monomials(relative):
    powers = []
    for column in range(3):
        base = relative[column]
        square = base * base
        powers.append([jnp.ones_like(base), base, square, square * base, square * square])
    return jnp.stack([powers[0][first] * powers[1][second] * powers[2][third] for first, second, third in exponent_list()])

def crossed(left, right):
    return jnp.stack([left[1] * right[2] - left[2] * right[1], left[2] * right[0] - left[0] * right[2], left[0] * right[1] - left[1] * right[0]])

def pair_forces(target, source, shift):
    separation = [shift[column] + source[column][..., None, :] - target[column][..., :, None] for column in range(3)]
    radius_sq = separation[0] * separation[0] + separation[1] * separation[1] + separation[2] * separation[2] + core_square
    inverse = 1.0 / (radius_sq * jnp.sqrt(radius_sq))
    burgers_dot = sum((target[6 + column][..., :, None] * source[6 + column][..., None, :] for column in range(3)))
    line_dot = sum((target[3 + column][..., :, None] * source[3 + column][..., None, :] for column in range(3)))
    target_proj = sum((target[6 + column][..., :, None] * separation[column] for column in range(3)))
    source_proj = sum((source[6 + column][..., None, :] * separation[column] for column in range(3)))
    first_coef = inverse * burgers_dot * line_dot
    second_coef = inverse * target_proj * source_proj / radius_sq
    return jnp.stack([lax.optimization_barrier(jnp.sum(first_coef * separation[column] + second_coef * source[3 + column][..., None, :], -1)) for column in range(3)])

def near_total(inner, padded):
    extent = inner.shape[1:4]
    total = jnp.zeros((3,) + inner.shape[1:], jnp.float32)
    for step_x in (-1, 0, 1):
        for step_y in (-1, 0, 1):
            for step_z in (-1, 0, 1):
                source = padded[:, 1 + step_x:1 + step_x + extent[0], 1 + step_y:1 + step_y + extent[1], 1 + step_z:1 + step_z + extent[2]]
                total = total + pair_forces(inner, source, (float(step_x), float(step_y), float(step_z)))
    return near_scale * total

def cell_moments(poly, charge, slots, width):
    moments = jnp.einsum('kxyzs,cxyzs->xyzck', poly, charge, precision=highest) / slots
    flat = moments.reshape(-1, 3 * poly.shape[0])
    return jnp.pad(flat, ((0, 0), (0, width - flat.shape[1])))

def far_weights(rows_first, rows_second, extents):
    total_sq = jnp.zeros((rows_first[0].shape[0], rows_second[0].shape[0]), jnp.float32)
    largest = jnp.zeros((rows_first[0].shape[0], rows_second[0].shape[0]), jnp.int32)
    for column in range(3):
        spacing = jnp.abs(rows_first[column][:, None] - rows_second[column][None, :]) % extents[column]
        spacing = jnp.minimum(spacing, extents[column] - spacing)
        largest = jnp.maximum(largest, spacing)
        total_sq = total_sq + spacing.astype(jnp.float32) * spacing.astype(jnp.float32)
    return jnp.where(largest > 1, 1.0 / jnp.sqrt(jnp.maximum(total_sq, 1.0)), 0.0).astype(jnp.float32)

def finish(lines, charge, mask, poly, near, coefficients, mobility, stress):
    terms = poly.shape[0]
    blocks = coefficients[..., :3 * terms].reshape(coefficients.shape[:3] + (3, terms))
    far = jnp.einsum('kxyzs,xyzak->axyzs', poly, blocks, precision=highest)
    stressed = jnp.stack([sum((stress[row, column] * charge[column] for column in range(3))) for row in range(3)])
    applied = crossed(stressed, lines)
    force = near + far * mask + applied
    along = lax.optimization_barrier(jnp.sum(force * lines, 0)) / jnp.maximum(lax.optimization_barrier(jnp.sum(lines * lines, 0)), 1.0)
    return mobility[..., None] * mask * (force - along * lines)

def reference(offsets, lines, burgers, counts, mobility, stress, translation):
    slots = offsets.shape[-1]
    mask = (lax.broadcasted_iota(jnp.int32, counts.shape + (slots,), 3) < counts[..., None]).astype(jnp.float32)
    charge = burgers * mask
    stacked = jnp.concatenate([offsets, lines, charge], 0)
    padded = jnp.pad(stacked, ((0, 0), (1, 1), (1, 1), (1, 1), (0, 0)), mode='wrap')

    def slab_force(index):
        slab = lax.dynamic_slice_in_dim(padded, index, 3, 1)
        return near_total(slab[:, 1:2, 1:-1, 1:-1], slab)
    near = lax.map(slab_force, jnp.arange(NCX, dtype=jnp.int32))
    near = jnp.moveaxis(near[:, :, 0], 0, 1)
    poly = monomials(offsets)
    moments = cell_moments(poly, crossed(charge, lines), slots, translation.shape[0])
    cell_index = jnp.arange(CELLS, dtype=jnp.int32)
    columns = (cell_index // (NCY * NCZ), cell_index // NCZ % NCY, cell_index % NCZ)
    block = math.gcd(CELLS, 512)

    def expand(start):
        rows = start + jnp.arange(block, dtype=jnp.int32)
        weights = far_weights((rows // (NCY * NCZ), rows // NCZ % NCY, rows % NCZ), columns, (NCX, NCY, NCZ))
        return jnp.dot(weights, moments, precision=highest, preferred_element_type=jnp.float32)
    local = lax.map(expand, jnp.arange(0, CELLS, block, dtype=jnp.int32)).reshape(CELLS, -1)
    coefficients = jnp.dot(local, translation, precision=highest, preferred_element_type=jnp.float32)
    coefficients = coefficients.reshape(NCX, NCY, NCZ, -1)
    return finish(lines, charge, mask, poly, near, coefficients, mobility, stress)
```

```python
import functools
import itertools
import math

import jax
import jax.numpy as jnp
import numpy as np
from jax import lax
from jax.experimental import pallas as pl
from jax.experimental.pallas import tpu as pltpu
from jax.sharding import PartitionSpec as P

core_square = 0.0625
near_scale = 0.01
highest = lax.Precision.HIGHEST
f32 = jnp.float32
bf16 = jnp.bfloat16
slots = 128
cells = 8
features = 64
forms = 4


def exponent_list():
    result = []
    for first in range(5):
        for second in range(5 - first):
            for third in range(5 - first - second):
                result.append((first, second, third))
    return result


def monomials(relative):
    powers = []
    for base in relative:
        square = base * base
        powers.append([None, base, square, square * base, square * square])
    result = []
    for triple in exponent_list():
        factors = [powers[axis][power] for axis, power in enumerate(triple) if power]
        result.append(functools.reduce(lambda a, b: a * b, factors) if factors else None)
    return result


def crossed(left, right):
    return [
        left[1] * right[2] - left[2] * right[1],
        left[2] * right[0] - left[0] * right[2],
        left[0] * right[1] - left[1] * right[0],
    ]


def dotted(left, right):
    return left[0] * right[0] + left[1] * right[1] + left[2] * right[2]


def split(value, parts):
    result = []
    for _ in range(parts):
        part = value.astype(bf16).astype(f32)
        result.append(part)
        value = value - part
    return result


def by_cell(scalars):
    row = lax.broadcasted_iota(jnp.int32, (cells, slots), 0)
    result = jnp.full((cells, slots), scalars[0, 0, 0])
    for cell in range(1, cells):
        result = jnp.where(row == cell, scalars[cell // 4, cell // 2 % 2, cell % 2], result)
    return result


def prepare_kernel(counts, offsets, lines, burgers, translation, out, after, before, alone):
    slot = lax.broadcasted_iota(jnp.int32, (cells, slots), 1)
    mask = (slot < by_cell(counts)).astype(f32)
    place = [offsets[axis] for axis in range(3)]
    line = [lines[axis] for axis in range(3)]
    charge = [burgers[axis] * mask for axis in range(3)]
    for axis in range(3):
        out[axis] = place[axis]
        out[3 + axis] = line[axis]
        out[6 + axis] = charge[axis]
    strength = crossed(charge, line)
    poly = monomials(place)
    moments = jnp.zeros((cells, slots), f32)
    for axis in range(3):
        for term, value in enumerate(poly):
            weighted = strength[axis] if value is None else value * strength[axis]
            total = jnp.sum(weighted, axis=1, keepdims=True)
            moments = jnp.where(slot == axis * len(poly) + term, total, moments)
    moved = jnp.dot(
        moments * (1.0 / slots), translation[...], precision=highest, preferred_element_type=f32
    )
    out[9] = moved
    alone[...] = moved
    for plane, message in ((0, after), (1, before)):
        for index in range(4):
            cell = 2 * index + plane
            message[0:9, index : index + 1, :] = out[0:9, cell : cell + 1, :]
        message[9] = moved[:4]
        message[10] = moved[4:]


def stack_rows(message, pieces, width):
    row = 0
    for piece in pieces:
        count = piece.shape[0]
        layer, start = (9 + row // width, row % width)
        message[layer, start : start + count, :] = piece
        row += count


def pack_x_kernel(own, high, low, *rest):
    middle, message = (rest[:-2], rest[-1])
    message[0:9, 0:8, :] = own[0:9]
    message[0:9, 8:12, :] = high[0:9]
    message[0:9, 12:16, :] = low[0:9]
    pieces = [own[9], high[9], high[10]] + [piece[...] for piece in middle] + [low[9], low[10]]
    stack_rows(message, pieces, 16)


def pack_y_kernel(starts, inner, outer, *rest):
    tails, messages, alone = (rest[: len(starts)], rest[-3:-1], rest[-1])
    for plane, message in enumerate(messages):
        for index, block in enumerate((inner, outer)):
            first = 8 * index
            for half in range(2):
                here, there = (first + 2 * half, 4 * half + 2 * plane)
                message[0:9, here : here + 2, :] = block[0:9, there : there + 2, :]
            for line in range(4):
                here, there = (first + 4 + line, 8 + 2 * line + plane)
                message[0:9, here : here + 1, :] = block[0:9, there : there + 1, :]
        layer = 9
        for start, tail in zip(starts, tails):
            for index in range(start, tail.shape[0]):
                message[layer] = tail[index]
                alone[layer - 9] = tail[index]
                layer += 1


def target_rows(place, line, charge):
    one = jnp.ones_like(place[0])
    rows = []
    for axis in range(3):
        high, middle, low = split(place[axis], 3)
        rows += [high, high, high, middle, middle, low]
    rows += split(dotted(place, place), 3)
    rows += [one, one, one]
    for axis in range(3):
        high, low = split(charge[axis], 2)
        rows += [high, high, low]
    rows += split(dotted(charge, place), 3)
    for first in range(3):
        for second in range(3):
            high, low = split(charge[first] * line[second], 2)
            rows += [high, high, low]
    return rows + [jnp.zeros_like(one)]


def source_rows(place, line, charge):
    one = jnp.ones_like(place[0])
    none = None
    radius, product, own, other = ([], [], [], [])
    for axis in range(3):
        high, middle, low = split(-2.0 * place[axis], 3)
        radius += [high, middle, low, high, middle, high]
        high, middle, low = split(charge[axis], 3)
        own += [high, middle, low, high, middle, high]
    product += [none] * 18
    other += [none] * 18
    radius += [one, one, one]
    own += [none] * 3
    product += [none] * 3
    other += [none] * 3
    radius += split(dotted(place, place) + core_square, 3)
    own += split(-dotted(charge, place), 3)
    product += [none] * 3
    other += [none] * 3
    for axis in range(3):
        high, low = split(-place[axis], 2)
        other += [high, low, high]
    other += [one, one, one]
    radius += [none] * 12
    own += [none] * 12
    product += [none] * 12
    for first in range(3):
        for second in range(3):
            high, low = split(charge[first] * line[second], 2)
            product += [high, low, high]
    product += [none]
    radius += [none] * 28
    own += [none] * 28
    other += [none] * 28
    return [radius, product, own, other]


def moved_block(block, base):
    place = [block[axis] + base[axis] for axis in range(3)]
    return place, [block[3 + axis] for axis in range(3)], [block[6 + axis] for axis in range(3)]


def add_targets(block, base, targets, stage):
    for index, row in enumerate(target_rows(*moved_block(block, base))):
        stage[index * cells : (index + 1) * cells, :] = row
    for cell in range(cells):
        rows = stage[pl.ds(cell, features, stride=cells), :]
        targets[cell * slots : (cell + 1) * slots, :] = rows.T.astype(bf16)


def add_sources(block, base, columns, parts, positions, stage):
    place, line, charge = moved_block(block, base)
    for form, rows in enumerate(source_rows(place, line, charge)):
        used = [index for index, row in enumerate(rows) if row is not None]
        low, high = (min(used) // 16 * 16, -(-(max(used) + 1) // 16) * 16)
        for index in range(low, high):
            row = jnp.zeros((cells, slots), f32) if rows[index] is None else rows[index]
            stage[index * cells : (index + 1) * cells, :] = row
        for cell in range(cells):
            part = stage[pl.ds(low * cells + cell, high - low, stride=cells), :].astype(bf16)
            first = (positions[cell] * forms + form) * slots
            if low:
                columns[0:low, first : first + slots] = jnp.zeros((low, slots), bf16)
            columns[low:high, first : first + slots] = part
            if high < features:
                rest = jnp.zeros((features - high, slots), bf16)
                columns[high:features, first : first + slots] = rest
    for index, row in enumerate(place + line):
        stage[index * cells : (index + 1) * cells, :] = row
    for cell in range(cells):
        first = positions[cell] * 8
        parts[first : first + 8, :] = stage[pl.ds(cell, 8, stride=cells), :]


def pair_products(mine, columns, first, count):
    width = forms * slots
    start = pl.multiple_of(first * width, width)
    return jnp.dot(mine, columns[:, pl.ds(start, count * width)], preferred_element_type=f32)


def add_pairs(totals, value, parts, first, count, fresh):
    start = pl.multiple_of(first * 8, 8)
    sources = []
    for cell in range(count):
        rows = parts[pl.ds(start + cell * 8, 8), :]
        sources.append([jnp.broadcast_to(rows[i : i + 1], (8, slots)) for i in range(6)])
    for group in range(value.shape[0] // 8):
        here = slice(group * 8, group * 8 + 8)
        sums = [None] * 4
        for cell in range(count):
            radius, product, own, other = (
                value[here, (cell * forms + form) * slots : (cell * forms + form + 1) * slots]
                for form in range(forms)
            )
            inverse = lax.rsqrt(radius)
            square = inverse * inverse
            cube = inverse * square
            along = product * cube
            across = (own * other) * (square * cube)
            terms = [along * sources[cell][a] + across * sources[cell][3 + a] for a in range(3)]
            terms.append(along)
            sums = [term if s is None else s + term for s, term in zip(sums, terms)]
        for index in range(4):
            place = slice(index * slots + group * 8, index * slots + group * 8 + 8)
            totals[place, :] = sums[index] if fresh else totals[place, :] + sums[index]


def own_cells():
    return [(x + 1, y + 1, z + 1) for x in range(2) for y in range(2) for z in range(2)]


def z_cells():
    return [(x + 1, y + 1, z) for z in (3, 0) for x in range(2) for y in range(2)]


def x_cells():
    near = [(x, y + 1, z + 1) for x in (3, 0) for y in range(2) for z in range(2)]
    return [near, [(x, y + 1, z) for z in (3, 0) for x in (3, 0) for y in range(2)]]


def y_cells(y):
    result = []
    for xs in ((1, 2), (3, 0)):
        cell = [(x, y, z + 1) for x in xs for z in range(2)]
        result.append(cell + [(x, y, z) for z in (3, 0) for x in xs])
    return result


def base_of(places):
    row = lax.broadcasted_iota(jnp.int32, (cells, slots), 0)
    result = []
    for axis in range(3):
        value = jnp.full((cells, slots), places[0][axis] - 1.5, f32)
        for cell in range(1, cells):
            if places[cell][axis] != places[0][axis]:
                value = jnp.where(row == cell, places[cell][axis] - 1.5, value)
        result.append(value)
    return result


def near_sums(targets, groups, runs_of, earlier, columns, parts, stage, totals, mixed, gathered):
    for block, places, positions in groups:
        add_sources(block, base_of(places), columns, parts, positions, stage)

    def one_target(target, carry):
        mine = targets[pl.ds(pl.multiple_of(target * slots, slots), slots), :]
        runs = runs_of(target // 4, target // 2 % 2, target % 2)
        value = pair_products(mine, columns, *runs[0])
        for index, run in enumerate(runs):
            later = None
            if index + 1 < len(runs):
                later = pair_products(mine, columns, *runs[index + 1])
            add_pairs(totals, value, parts, *run, index == 0)
            value = later
        lane = lax.broadcasted_iota(jnp.int32, (slots, slots), 1)
        for index in range(4):
            total = jnp.sum(totals[index * slots : (index + 1) * slots, :], axis=1, keepdims=True)
            mixed[...] = jnp.where(lane == index * cells + target, total, mixed[...])
        return carry

    mixed[...] = jnp.zeros((slots, slots), f32)
    lax.fori_loop(0, cells, one_target, 0)
    result = mixed[...].T[: 4 * cells, :]
    gathered[...] = result if earlier is None else result + earlier[...]


def rows_of(block, first=0):
    return [block[axis, first : first + cells, :] for axis in range(9)]


def own_kernel(own, message, targets, out, *scratch):
    add_targets(rows_of(own), base_of(own_cells()), targets, scratch[2])
    groups = [(rows_of(own), own_cells(), list(range(8)))]

    def runs(x, y, z):
        return [(first, 2) for first in (0, 2, 4, 6)]

    near_sums(targets, groups, runs, None, *scratch, out)


def z_kernel(targets, halo, earlier, out, *scratch):
    groups = [(rows_of(halo, 8), z_cells(), list(range(8)))]

    def runs(x, y, z):
        return [(4 * (1 - z) + first, 2) for first in (0, 2)]

    near_sums(targets, groups, runs, earlier, *scratch, out)


def x_kernel(targets, halo, message, earlier, out, *scratch):
    groups = []
    for index, places in enumerate(x_cells()):
        positions = [(0 if x == 3 else 8) + 2 * z + y - 1 for x, y, z in places]
        groups.append((rows_of(halo, 8 * index), places, positions))

    def runs(x, y, z):
        return [(8 * (1 - x) + 2 * z + first, 2) for first in (0, 2, 4)]

    near_sums(targets, groups, runs, earlier, *scratch, out)


def y_kernel(
    starts, stress, mobility, counts, own, targets, high, low, earlier, weights_far, *rest
):
    tails, out, scratch = (rest[: len(starts)], rest[len(starts)], rest[len(starts) + 1 :])
    gathered = scratch[-1]
    groups = []
    for block, side in ((high, 3), (low, 0)):
        for index, places in enumerate(y_cells(side)):
            positions = [(16 if side else 0) + 4 * x + z for x, y, z in places]
            groups.append((rows_of(block, 8 * index), places, positions))

    def runs(x, y, z):
        return [(16 * y + 4 * (x + line) + z, 3) for line in range(3)]

    near_sums(targets, groups, runs, earlier, *scratch)
    sums_of = [gathered[index * cells : (index + 1) * cells, :] for index in range(4)]
    local = [tail[index] for start, tail in zip(starts, tails) for index in range(start, tail.shape[0])]
    coefficients = jnp.dot(
        weights_far[...],
        jnp.concatenate(local, axis=0),
        precision=highest,
        preferred_element_type=f32,
    )
    place = [own[axis] for axis in range(3)]
    line = [own[3 + axis] for axis in range(3)]
    charge = [own[6 + axis] for axis in range(3)]
    base = base_of(own_cells())
    poly = monomials(place)
    mask = (lax.broadcasted_iota(jnp.int32, (cells, slots), 1) < by_cell(counts)).astype(f32)
    stressed = [
        stress[a, 0] * charge[0] + stress[a, 1] * charge[1] + stress[a, 2] * charge[2]
        for a in range(3)
    ]
    applied = crossed(stressed, line)
    force = []
    for axis in range(3):
        at = place[axis] + base[axis]
        near = sums_of[axis] - at * sums_of[3]
        far = jnp.zeros((cells, slots), f32)
        for term, value in enumerate(poly):
            column = axis * len(poly) + term
            coefficient = coefficients[:, column : column + 1]
            far = far + (coefficient if value is None else coefficient * value)
        force.append(near_scale * near + far * mask + applied[axis])
    ratio = dotted(force, line) / jnp.maximum(dotted(line, line), 1.0)
    scale = by_cell(mobility) * mask
    for axis in range(3):
        out[axis] = scale * (force[axis] - ratio * line[axis])


def far_weights(sizes):
    corners = list(itertools.product(range(2), repeat=3))
    result = []
    for here in corners:
        line = []
        for y, x, z in itertools.product(range(sizes[1]), range(sizes[0]), range(sizes[2])):
            for there in corners:
                gaps = []
                for axis, step in enumerate((x, y, z)):
                    extent = 2 * sizes[axis]
                    gap = (2 * step + there[axis] - here[axis]) % extent
                    gaps.append(min(gap, extent - gap))
                apart = math.sqrt(sum(gap * gap for gap in gaps))
                line.append(1.0 / apart if max(gaps) > 1 else 0.0)
        result.append(line)
    return np.asarray(result, np.float32)


def shifted(value, axis, step):
    count = lax.axis_size(axis)
    return lax.ppermute(value, axis, [(i, (i - step) % count) for i in range(count)])


def near_call(kernel, name, count, pairs, scalars, arrays, shape, last=False):
    vmem = pl.BlockSpec(memory_space=pltpu.VMEM)
    smem = pl.BlockSpec(memory_space=pltpu.SMEM)
    scratch = [
        pltpu.VMEM((features, count * forms * slots), bf16),
        pltpu.VMEM((count * 8, slots), f32),
        pltpu.VMEM((features * cells, slots), f32),
        pltpu.VMEM((4 * slots, slots), f32),
        pltpu.VMEM((slots, slots), f32),
    ]
    if last:
        scratch.append(pltpu.VMEM((4 * cells, slots), f32))
    return pl.pallas_call(
        kernel,
        out_shape=shape,
        in_specs=[smem] * len(scalars) + [vmem] * len(arrays),
        out_specs=jax.tree.map(lambda leaf: vmem, shape),
        scratch_shapes=scratch,
        compiler_params=pltpu.CompilerParams(vmem_limit_bytes=8 * 1024 * 1024),
        cost_estimate=pl.CostEstimate(
            flops=pairs * slots * slots * 8000, bytes_accessed=1 << 20, transcendentals=0
        ),
        name=name,
    )(*scalars, *arrays)


def body(offsets, lines, burgers, counts, mobility, stress, translation):
    sizes = [lax.axis_size(axis) for axis in ("gx", "gy", "gz")]
    flat = [value.reshape(3, cells, slots) for value in (offsets, lines, burgers)]
    vmem = pl.BlockSpec(memory_space=pltpu.VMEM)
    smem = pl.BlockSpec(memory_space=pltpu.SMEM)
    message = jax.ShapeDtypeStruct((11, 4, slots), f32)
    block = jax.ShapeDtypeStruct((10, cells, slots), f32)
    own, up, down, moments = pl.pallas_call(
        prepare_kernel,
        out_shape=(block, message, message, jax.ShapeDtypeStruct((cells, slots), f32)),
        in_specs=[smem] + [vmem] * 4,
        out_specs=(vmem,) * 4,
        compiler_params=pltpu.CompilerParams(vmem_limit_bytes=4 * 1024 * 1024),
        name="prepare",
    )(counts, *flat, translation)
    high = shifted(up, "gz", 1)
    low = shifted(down, "gz", -1)
    middle = [shifted(moments, "gz", step) for step in range(2, sizes[2] - 1)]
    sums = jax.ShapeDtypeStruct((4 * cells, slots), f32)
    both = (jax.ShapeDtypeStruct((cells * slots, features), bf16), sums)
    targets, partial = near_call(own_kernel, "near_own", 8, 64, [], [own, up], both)
    message = pl.pallas_call(
        pack_x_kernel,
        out_shape=jax.ShapeDtypeStruct((9 + sizes[2] // 2, 16, slots), f32),
        in_specs=[vmem] * (4 + len(middle)),
        out_specs=vmem,
        compiler_params=pltpu.CompilerParams(vmem_limit_bytes=4 * 1024 * 1024),
        name="pack_x",
    )(own, high, low, *middle, partial)
    if sizes[0] == 2:
        outer = shifted(message, "gx", 1)
        starts, tails = ([9, 9], [message, outer])
    else:
        moments = message[9:].reshape(-1, slots)
        tail = moments.reshape(-1, 8, slots)
        planes = []
        for plane in (0, 1):
            part = [
                message[:9, :8].reshape(9, 2, 4, slots)[:, plane],
                message[:9, 8:].reshape(9, 2, 2, 2, slots)[:, :, plane].reshape(9, 4, slots),
            ]
            planes.append(jnp.concatenate([jnp.concatenate(part, axis=1), tail], axis=0))
        after = shifted(planes[0], "gx", 1)
        before = shifted(planes[1], "gx", -1)
        others = [shifted(moments, "gx", step) for step in range(2, sizes[0] - 1)]
        both = [after[:9], before[:9]]
        sides = [value[:, 4:].reshape(9, 2, 1, 2, slots) for value in both]
        sides = jnp.concatenate(sides, axis=2).reshape(9, 8, slots)
        outer = jnp.concatenate([value[:, :4] for value in both] + [sides], axis=1)
        moments = jnp.concatenate(
            [moments, after[9:].reshape(-1, slots)] + others + [before[9:].reshape(-1, slots)],
            axis=0,
        )
        starts, tails = ([0], [moments.reshape(-1, 16, slots)])
    partial = near_call(z_kernel, "near_z", 8, 32, [], [targets, message, partial], sums)
    layers = 9 + sum(tail.shape[0] - start for start, tail in zip(starts, tails))
    face = jax.ShapeDtypeStruct((layers, 16, slots), f32)
    up, down, moments = pl.pallas_call(
        functools.partial(pack_y_kernel, starts),
        out_shape=(face, face, jax.ShapeDtypeStruct((layers - 9, 16, slots), f32)),
        in_specs=[vmem] * (3 + len(tails)),
        out_specs=(vmem,) * 3,
        compiler_params=pltpu.CompilerParams(vmem_limit_bytes=4 * 1024 * 1024),
        name="pack_y",
    )(message, outer, *tails, partial)
    high = shifted(up, "gy", 1)
    low = shifted(down, "gy", -1)
    middle = [shifted(moments, "gy", step) for step in range(2, sizes[1] - 1)]
    partial = near_call(x_kernel, "near_x", 16, 48, [], [targets, outer, up, partial], sums)
    starts = starts + [9] + [0] * len(middle) + [9]
    tails = tails + [high] + middle + [low]
    out = near_call(
        functools.partial(y_kernel, starts),
        "near_y",
        32,
        72,
        [stress, mobility, counts],
        [own, targets, high, low, partial, jnp.asarray(far_weights(sizes))] + tails,
        jax.ShapeDtypeStruct((3, cells, slots), f32),
        last=True,
    )
    return out.reshape(3, 2, 2, 2, slots)


def solution(mesh):
    placed = (
        P(None, "gx", "gy", "gz", None),
        P(None, "gx", "gy", "gz", None),
        P(None, "gx", "gy", "gz", None),
        P("gx", "gy", "gz"),
        P("gx", "gy", "gz"),
        P(),
        P(),
    )
    return jax.shard_map(
        body, mesh=mesh, in_specs=placed, out_specs=P(None, "gx", "gy", "gz", None), check_vma=False
    )
```

```python
import functools
import itertools
import math

import jax
import jax.numpy as jnp
import numpy as np
from jax import lax
from jax.experimental import pallas as pl
from jax.experimental.pallas import tpu as pltpu
from jax.sharding import PartitionSpec as P

core_square = 0.0625
near_scale = 0.01
highest = lax.Precision.HIGHEST
f32 = jnp.float32
bf16 = jnp.bfloat16
slots = 128
cells = 8
features = 64
forms = 4


def exponent_list():
    result = []
    for first in range(5):
        for second in range(5 - first):
            for third in range(5 - first - second):
                result.append((first, second, third))
    return result


def monomials(relative):
    powers = []
    for base in relative:
        square = base * base
        powers.append([None, base, square, square * base, square * square])
    result = []
    for triple in exponent_list():
        factors = [powers[axis][power] for axis, power in enumerate(triple) if power]
        result.append(functools.reduce(lambda a, b: a * b, factors) if factors else None)
    return result


def crossed(left, right):
    return [
        left[1] * right[2] - left[2] * right[1],
        left[2] * right[0] - left[0] * right[2],
        left[0] * right[1] - left[1] * right[0],
    ]


def dotted(left, right):
    return left[0] * right[0] + left[1] * right[1] + left[2] * right[2]


def split(value, parts):
    result = []
    for _ in range(parts):
        part = value.astype(bf16).astype(f32)
        result.append(part)
        value = value - part
    return result


def by_cell(scalars):
    row = lax.broadcasted_iota(jnp.int32, (cells, slots), 0)
    result = jnp.full((cells, slots), scalars[0, 0, 0])
    for cell in range(1, cells):
        result = jnp.where(row == cell, scalars[cell // 4, cell // 2 % 2, cell % 2], result)
    return result


def prepare_kernel(counts, segments, out, after, before, alone):
    slot = lax.broadcasted_iota(jnp.int32, (cells, slots), 1)
    mask = (slot < by_cell(counts)).astype(f32)
    place = [segments[axis] for axis in range(3)]
    line = [segments[3 + axis] for axis in range(3)]
    charge = [segments[6 + axis] * mask for axis in range(3)]
    out[0:6] = segments[0:6]
    for axis in range(3):
        out[6 + axis] = charge[axis]
    strength = crossed(charge, line)
    poly = monomials(place)
    moments = jnp.zeros((cells, slots), f32)
    for axis in range(3):
        for term, value in enumerate(poly):
            weighted = strength[axis] if value is None else value * strength[axis]
            total = jnp.sum(weighted, axis=1, keepdims=True)
            moments = jnp.where(slot == axis * len(poly) + term, total, moments)
    moved = moments * (1.0 / slots)
    out[9] = moved
    alone[...] = moved
    for plane, message in ((0, after), (1, before)):
        for index in range(4):
            cell = 2 * index + plane
            message[0:9, index : index + 1, :] = out[0:9, cell : cell + 1, :]
        message[9] = moved[:4]
        message[10] = moved[4:]


def stack_rows(message, pieces, width):
    row = 0
    for piece in pieces:
        count = piece.shape[0]
        layer, start = (9 + row // width, row % width)
        message[layer, start : start + count, :] = piece
        row += count


def pack_x_kernel(own, high, low, *rest):
    middle, message = (rest[:-2], rest[-1])
    message[0:9, 0:8, :] = own[0:9]
    message[0:9, 8:12, :] = high[0:9]
    message[0:9, 12:16, :] = low[0:9]
    pieces = [own[9], high[9], high[10]] + [piece[...] for piece in middle] + [low[9], low[10]]
    stack_rows(message, pieces, 16)


def pack_y_kernel(starts, inner, outer, *rest):
    tails, messages, alone = (rest[: len(starts)], rest[-3:-1], rest[-1])
    for plane, message in enumerate(messages):
        for index, block in enumerate((inner, outer)):
            first = 8 * index
            for half in range(2):
                here, there = (first + 2 * half, 4 * half + 2 * plane)
                message[0:9, here : here + 2, :] = block[0:9, there : there + 2, :]
            for line in range(4):
                here, there = (first + 4 + line, 8 + 2 * line + plane)
                message[0:9, here : here + 1, :] = block[0:9, there : there + 1, :]
        layer = 9
        for start, tail in zip(starts, tails):
            for index in range(start, tail.shape[0]):
                message[layer] = tail[index]
                alone[layer - 9] = tail[index]
                layer += 1


def target_rows(place, line, charge):
    one = jnp.ones_like(place[0])
    rows = []
    for axis in range(3):
        high, middle, low = split(place[axis], 3)
        rows += [high, high, high, middle, middle, low]
    rows += split(dotted(place, place), 3)
    rows += [one, one, one]
    for axis in range(3):
        high, low = split(charge[axis], 2)
        rows += [high, high, low]
    rows += split(dotted(charge, place), 3)
    for first in range(3):
        for second in range(3):
            high, low = split(charge[first] * line[second], 2)
            rows += [high, high, low]
    return rows + [jnp.zeros_like(one)]


def source_rows(place, line, charge):
    one = jnp.ones_like(place[0])
    none = None
    radius, product, own, other = ([], [], [], [])
    for axis in range(3):
        high, middle, low = split(-2.0 * place[axis], 3)
        radius += [high, middle, low, high, middle, high]
        high, middle, low = split(charge[axis], 3)
        own += [high, middle, low, high, middle, high]
    product += [none] * 18
    other += [none] * 18
    radius += [one, one, one]
    own += [none] * 3
    product += [none] * 3
    other += [none] * 3
    radius += split(dotted(place, place) + core_square, 3)
    own += split(-dotted(charge, place), 3)
    product += [none] * 3
    other += [none] * 3
    for axis in range(3):
        high, low = split(-place[axis], 2)
        other += [high, low, high]
    other += [one, one, one]
    radius += [none] * 12
    own += [none] * 12
    product += [none] * 12
    for first in range(3):
        for second in range(3):
            high, low = split(charge[first] * line[second], 2)
            product += [high, low, high]
    product += [none]
    radius += [none] * 28
    own += [none] * 28
    other += [none] * 28
    return [radius, product, own, other]


def moved_block(block, base):
    place = [block[axis] + base[axis] for axis in range(3)]
    return place, [block[3 + axis] for axis in range(3)], [block[6 + axis] for axis in range(3)]


def target_order():
    return [4 * x + 2 * y + z for x in range(2) for z in range(2) for y in range(2)]


def add_targets(block, base, targets, stage):
    for index, row in enumerate(target_rows(*moved_block(block, base))):
        stage[index * cells : (index + 1) * cells, :] = row
    for position, cell in enumerate(target_order()):
        rows = stage[pl.ds(cell, features, stride=cells), :]
        targets[position * slots : (position + 1) * slots, :] = rows.T.astype(bf16)


def add_sources(block, base, columns, parts, positions, stage):
    place, line, charge = moved_block(block, base)
    for form, rows in enumerate(source_rows(place, line, charge)):
        used = [index for index, row in enumerate(rows) if row is not None]
        low, high = (min(used) // 16 * 16, -(-(max(used) + 1) // 16) * 16)
        for index in range(low, high):
            row = jnp.zeros((cells, slots), f32) if rows[index] is None else rows[index]
            stage[index * cells : (index + 1) * cells, :] = row
        for cell in range(cells):
            part = stage[pl.ds(low * cells + cell, high - low, stride=cells), :].astype(bf16)
            first = (positions[cell] * forms + form) * slots
            if low:
                columns[0:low, first : first + slots] = jnp.zeros((low, slots), bf16)
            columns[low:high, first : first + slots] = part
            if high < features:
                rest = jnp.zeros((features - high, slots), bf16)
                columns[high:features, first : first + slots] = rest
    for index, row in enumerate(place + line):
        stage[index * cells : (index + 1) * cells, :] = row
    for cell in range(cells):
        first = positions[cell] * 8
        parts[first : first + 8, :] = stage[pl.ds(cell, 8, stride=cells), :]


def pair_products(mine, columns, first, count):
    width = forms * slots
    start = pl.multiple_of(first * width, width)
    return jnp.dot(mine, columns[:, pl.ds(start, count * width)], preferred_element_type=f32)


def add_pairs(before, after, row, value, parts, first, count):
    start = pl.multiple_of(first * 8, 8)
    sources = []
    for cell in range(count):
        rows = parts[pl.ds(start + cell * 8, 8), :]
        sources.append([jnp.broadcast_to(rows[i : i + 1], (8, slots)) for i in range(6)])
    for group in range(value.shape[0] // 8):
        here = slice(group * 8, group * 8 + 8)
        sums = [None] * 4
        for cell in range(count):
            radius, product, own, other = (
                value[here, (cell * forms + form) * slots : (cell * forms + form + 1) * slots]
                for form in range(forms)
            )
            inverse = lax.rsqrt(radius)
            square = inverse * inverse
            cube = inverse * square
            along = product * cube
            across = (own * other) * (square * cube)
            terms = [along * sources[cell][a] + across * sources[cell][3 + a] for a in range(3)]
            terms.append(along)
            sums = [term if s is None else s + term for s, term in zip(sums, terms)]
        for index in range(4):
            place = pl.ds(pl.multiple_of(row + index * cells * slots + group * 8, 8), 8)
            after[place, :] = sums[index] if before is None else before[place, :] + sums[index]


def own_cells():
    return [(x + 1, y + 1, z + 1) for x in range(2) for y in range(2) for z in range(2)]


def z_cells():
    return [(x + 1, y + 1, z) for z in (3, 0) for x in range(2) for y in range(2)]


def x_cells():
    near = [(x, y + 1, z + 1) for x in (3, 0) for y in range(2) for z in range(2)]
    return [near, [(x, y + 1, z) for z in (3, 0) for x in (3, 0) for y in range(2)]]


def y_cells(y):
    result = []
    for xs in ((1, 2), (3, 0)):
        cell = [(x, y, z + 1) for x in xs for z in range(2)]
        result.append(cell + [(x, y, z) for z in (3, 0) for x in xs])
    return result


def base_of(places):
    row = lax.broadcasted_iota(jnp.int32, (cells, slots), 0)
    result = []
    for axis in range(3):
        value = jnp.full((cells, slots), places[0][axis] - 1.5, f32)
        for cell in range(1, cells):
            if places[cell][axis] != places[0][axis]:
                value = jnp.where(row == cell, places[cell][axis] - 1.5, value)
        result.append(value)
    return result


def near_sums(targets, groups, tasks_of, before, after, columns, parts, stage):
    for block, places, positions in groups:
        add_sources(block, base_of(places), columns, parts, positions, stage)

    def one_pair(pair, carry):
        tasks = tasks_of(pair // 2, pair % 2)

        def products(task):
            row = pl.multiple_of((pair * 2 + task[0]) * slots, slots)
            mine = targets[pl.ds(row, task[1] * slots), :]
            return row, pair_products(mine, columns, *task[2:])

        ready = products(tasks[0])
        seen = set()
        for index, task in enumerate(tasks):
            later = products(tasks[index + 1]) if index + 1 < len(tasks) else None
            earlier = after if task[0] in seen else before
            seen.add(task[0])
            add_pairs(earlier, after, *ready, parts, *task[2:])
            ready = later
        return carry

    lax.fori_loop(0, cells // 2, one_pair, 0)


def rows_of(block, first=0):
    return [block[axis, first : first + cells, :] for axis in range(9)]


def own_kernel(own, message, targets, sums, *scratch):
    add_targets(rows_of(own), base_of(own_cells()), targets, scratch[2])
    groups = [(rows_of(own), own_cells(), list(range(8)))]

    def tasks(x, z):
        return [(0, 2, first, 2) for first in (0, 2, 4, 6)]

    near_sums(targets, groups, tasks, None, sums, *scratch)


def z_kernel(targets, halo, before, after, *scratch):
    groups = [(rows_of(halo, 8), z_cells(), list(range(8)))]

    def tasks(x, z):
        return [(0, 2, 4 * (1 - z) + first, 2) for first in (0, 2)]

    near_sums(targets, groups, tasks, before, after, *scratch)


def x_kernel(targets, halo, message, before, after, *scratch):
    groups = []
    for index, places in enumerate(x_cells()):
        positions = [(0 if x == 3 else 8) + 2 * z + y - 1 for x, y, z in places]
        groups.append((rows_of(halo, 8 * index), places, positions))

    def tasks(x, z):
        return [(0, 2, 8 * (1 - x) + 2 * z + first, 2) for first in (0, 2, 4)]

    near_sums(targets, groups, tasks, before, after, *scratch)


def y_kernel(
    starts, stress, mobility, counts, own, targets, high, low, before, weights_far, translation, *rest
):
    tails, out, scratch = (rest[: len(starts)], rest[len(starts)], rest[len(starts) + 1 :])
    after = scratch[-1]
    groups = []
    for block, side in ((high, 3), (low, 0)):
        for index, places in enumerate(y_cells(side)):
            positions = [(16 if side else 0) + 4 * x + z for x, y, z in places]
            groups.append((rows_of(block, 8 * index), places, positions))

    def tasks(x, z):
        return [(y, 1, 16 * y + 4 * (x + line) + z, 3) for y in range(2) for line in range(3)]

    local = [tail[index] for start, tail in zip(starts, tails) for index in range(start, tail.shape[0])]
    coefficients = jnp.dot(
        weights_far[...],
        jnp.concatenate(local, axis=0),
        precision=highest,
        preferred_element_type=f32,
    )
    coefficients = jnp.dot(
        coefficients, translation[...], precision=highest, preferred_element_type=f32
    )
    place = [own[axis] for axis in range(3)]
    line = [own[3 + axis] for axis in range(3)]
    charge = [own[6 + axis] for axis in range(3)]
    base = base_of(own_cells())
    poly = monomials(place)
    mask = (lax.broadcasted_iota(jnp.int32, (cells, slots), 1) < by_cell(counts)).astype(f32)
    stressed = [
        stress[a, 0] * charge[0] + stress[a, 1] * charge[1] + stress[a, 2] * charge[2]
        for a in range(3)
    ]
    applied = crossed(stressed, line)
    outside = []
    for axis in range(3):
        far = jnp.zeros((cells, slots), f32)
        for term, value in enumerate(poly):
            column = axis * len(poly) + term
            coefficient = coefficients[:, column : column + 1]
            far = far + (coefficient if value is None else coefficient * value)
        outside.append(far * mask + applied[axis])
    scale = by_cell(mobility) * mask
    near_sums(targets, groups, tasks, before, after, *scratch[:-1])
    lane = lax.broadcasted_iota(jnp.int32, (slots, slots), 1)
    mixed = jnp.zeros((slots, slots), f32)
    for position, cell in enumerate(target_order()):
        for index in range(4):
            first = (index * cells + position) * slots
            total = jnp.sum(after[first : first + slots, :], axis=1, keepdims=True)
            mixed = jnp.where(lane == index * cells + cell, total, mixed)
    mixed = mixed.T
    sums_of = [mixed[index * cells : (index + 1) * cells, :] for index in range(4)]
    force = []
    for axis in range(3):
        at = place[axis] + base[axis]
        near = sums_of[axis] - at * sums_of[3]
        force.append(near_scale * near + outside[axis])
    ratio = dotted(force, line) / jnp.maximum(dotted(line, line), 1.0)
    for axis in range(3):
        out[axis] = scale * (force[axis] - ratio * line[axis])


def far_weights(sizes):
    corners = list(itertools.product(range(2), repeat=3))
    result = []
    for here in corners:
        line = []
        for y, x, z in itertools.product(range(sizes[1]), range(sizes[0]), range(sizes[2])):
            for there in corners:
                gaps = []
                for axis, step in enumerate((x, y, z)):
                    extent = 2 * sizes[axis]
                    gap = (2 * step + there[axis] - here[axis]) % extent
                    gaps.append(min(gap, extent - gap))
                apart = math.sqrt(sum(gap * gap for gap in gaps))
                line.append(1.0 / apart if max(gaps) > 1 else 0.0)
        result.append(line)
    return np.asarray(result, np.float32)


def shifted(value, axis, step):
    count = lax.axis_size(axis)
    return lax.ppermute(value, axis, [(i, (i - step) % count) for i in range(count)])


def near_call(kernel, name, count, pairs, scalars, arrays, shape, last=False):
    vmem = pl.BlockSpec(memory_space=pltpu.VMEM)
    smem = pl.BlockSpec(memory_space=pltpu.SMEM)
    scratch = [
        pltpu.VMEM((features, count * forms * slots), bf16),
        pltpu.VMEM((count * 8, slots), f32),
        pltpu.VMEM((features * cells, slots), f32),
    ]
    if last:
        scratch.append(pltpu.VMEM((4 * cells * slots, slots), f32))
    return pl.pallas_call(
        kernel,
        out_shape=shape,
        in_specs=[smem] * len(scalars) + [vmem] * len(arrays),
        out_specs=jax.tree.map(lambda leaf: vmem, shape),
        scratch_shapes=scratch,
        compiler_params=pltpu.CompilerParams(vmem_limit_bytes=8 * 1024 * 1024),
        cost_estimate=pl.CostEstimate(
            flops=pairs * slots * slots * 8000, bytes_accessed=1 << 20, transcendentals=0
        ),
        name=name,
    )(*scalars, *arrays)


def body(offsets, lines, burgers, counts, mobility, stress, translation):
    sizes = [lax.axis_size(axis) for axis in ("gx", "gy", "gz")]
    segments = jnp.concatenate([offsets, lines, burgers], axis=0).reshape(9, cells, slots)
    vmem = pl.BlockSpec(memory_space=pltpu.VMEM)
    smem = pl.BlockSpec(memory_space=pltpu.SMEM)
    message = jax.ShapeDtypeStruct((11, 4, slots), f32)
    block = jax.ShapeDtypeStruct((10, cells, slots), f32)
    own, up, down, moments = pl.pallas_call(
        prepare_kernel,
        out_shape=(block, message, message, jax.ShapeDtypeStruct((cells, slots), f32)),
        in_specs=[smem, vmem],
        out_specs=(vmem,) * 4,
        compiler_params=pltpu.CompilerParams(vmem_limit_bytes=4 * 1024 * 1024),
        name="prepare",
    )(counts, segments)
    high = shifted(up, "gz", 1)
    low = shifted(down, "gz", -1)
    middle = [shifted(moments, "gz", step) for step in range(2, sizes[2] - 1)]
    sums = jax.ShapeDtypeStruct((4 * cells * slots, slots), f32)
    both = (jax.ShapeDtypeStruct((cells * slots, features), bf16), sums)
    targets, partial = near_call(own_kernel, "near_own", 8, 64, [], [own, up], both)
    message = pl.pallas_call(
        pack_x_kernel,
        out_shape=jax.ShapeDtypeStruct((9 + sizes[2] // 2, 16, slots), f32),
        in_specs=[vmem] * (4 + len(middle)),
        out_specs=vmem,
        compiler_params=pltpu.CompilerParams(vmem_limit_bytes=4 * 1024 * 1024),
        name="pack_x",
    )(own, high, low, *middle, partial)
    if sizes[0] == 2:
        outer = shifted(message, "gx", 1)
        starts, tails = ([9, 9], [message, outer])
    else:
        moments = message[9:].reshape(-1, slots)
        tail = moments.reshape(-1, 8, slots)
        planes = []
        for plane in (0, 1):
            part = [
                message[:9, :8].reshape(9, 2, 4, slots)[:, plane],
                message[:9, 8:].reshape(9, 2, 2, 2, slots)[:, :, plane].reshape(9, 4, slots),
            ]
            planes.append(jnp.concatenate([jnp.concatenate(part, axis=1), tail], axis=0))
        after = shifted(planes[0], "gx", 1)
        before = shifted(planes[1], "gx", -1)
        others = [shifted(moments, "gx", step) for step in range(2, sizes[0] - 1)]
        both = [after[:9], before[:9]]
        sides = [value[:, 4:].reshape(9, 2, 1, 2, slots) for value in both]
        sides = jnp.concatenate(sides, axis=2).reshape(9, 8, slots)
        outer = jnp.concatenate([value[:, :4] for value in both] + [sides], axis=1)
        moments = jnp.concatenate(
            [moments, after[9:].reshape(-1, slots)] + others + [before[9:].reshape(-1, slots)],
            axis=0,
        )
        starts, tails = ([0], [moments.reshape(-1, 16, slots)])
    partial = near_call(z_kernel, "near_z", 8, 32, [], [targets, message, partial], sums)
    layers = 9 + sum(tail.shape[0] - start for start, tail in zip(starts, tails))
    face = jax.ShapeDtypeStruct((layers, 16, slots), f32)
    up, down, moments = pl.pallas_call(
        functools.partial(pack_y_kernel, starts),
        out_shape=(face, face, jax.ShapeDtypeStruct((layers - 9, 16, slots), f32)),
        in_specs=[vmem] * (3 + len(tails)),
        out_specs=(vmem,) * 3,
        compiler_params=pltpu.CompilerParams(vmem_limit_bytes=4 * 1024 * 1024),
        name="pack_y",
    )(message, outer, *tails, partial)
    high = shifted(up, "gy", 1)
    low = shifted(down, "gy", -1)
    middle = [shifted(moments, "gy", step) for step in range(2, sizes[1] - 1)]
    partial = near_call(x_kernel, "near_x", 16, 48, [], [targets, outer, up, partial], sums)
    starts = starts + [9] + [0] * len(middle) + [9]
    tails = tails + [high] + middle + [low]
    out = near_call(
        functools.partial(y_kernel, starts),
        "near_y",
        32,
        72,
        [stress, mobility, counts],
        [own, targets, high, low, partial, jnp.asarray(far_weights(sizes)), translation] + tails,
        jax.ShapeDtypeStruct((3, cells, slots), f32),
        last=True,
    )
    return out.reshape(3, 2, 2, 2, slots)


def solution(mesh):
    placed = (
        P(None, "gx", "gy", "gz", None),
        P(None, "gx", "gy", "gz", None),
        P(None, "gx", "gy", "gz", None),
        P("gx", "gy", "gz"),
        P("gx", "gy", "gz"),
        P(),
        P(),
    )
    return jax.shard_map(
        body, mesh=mesh, in_specs=placed, out_specs=P(None, "gx", "gy", "gz", None), check_vma=False
    )
```

```python
import functools
import itertools
import math

import jax
import jax.numpy as jnp
import numpy as np
from jax import lax
from jax.experimental import pallas as pl
from jax.experimental.pallas import tpu as pltpu
from jax.sharding import PartitionSpec as P

core_square = 0.0625
near_scale = 0.01
highest = lax.Precision.HIGHEST
f32 = jnp.float32
bf16 = jnp.bfloat16
slots = 128
cells = 8
features = 64
forms = 4


def exponent_list():
    result = []
    for first in range(5):
        for second in range(5 - first):
            for third in range(5 - first - second):
                result.append((first, second, third))
    return result


def monomials(relative):
    powers = []
    for base in relative:
        square = base * base
        powers.append([None, base, square, square * base, square * square])
    result = []
    for triple in exponent_list():
        factors = [powers[axis][power] for axis, power in enumerate(triple) if power]
        result.append(functools.reduce(lambda a, b: a * b, factors) if factors else None)
    return result


def crossed(left, right):
    return [
        left[1] * right[2] - left[2] * right[1],
        left[2] * right[0] - left[0] * right[2],
        left[0] * right[1] - left[1] * right[0],
    ]


def dotted(left, right):
    return left[0] * right[0] + left[1] * right[1] + left[2] * right[2]


def split(value, parts):
    result = []
    for _ in range(parts):
        part = value.astype(bf16).astype(f32)
        result.append(part)
        value = value - part
    return result


def by_cell(scalars):
    row = lax.broadcasted_iota(jnp.int32, (cells, slots), 0)
    result = jnp.full((cells, slots), scalars[0, 0, 0])
    for cell in range(1, cells):
        result = jnp.where(row == cell, scalars[cell // 4, cell // 2 % 2, cell % 2], result)
    return result


def prepare_kernel(counts, segments, out, after, before, alone):
    slot = lax.broadcasted_iota(jnp.int32, (cells, slots), 1)
    mask = (slot < by_cell(counts)).astype(f32)
    place = [segments[axis] for axis in range(3)]
    line = [segments[3 + axis] for axis in range(3)]
    charge = [segments[6 + axis] * mask for axis in range(3)]
    out[0:6] = segments[0:6]
    for axis in range(3):
        out[6 + axis] = charge[axis]
    strength = crossed(charge, line)
    poly = monomials(place)
    moments = jnp.zeros((cells, slots), f32)
    for axis in range(3):
        for term, value in enumerate(poly):
            weighted = strength[axis] if value is None else value * strength[axis]
            total = jnp.sum(weighted, axis=1, keepdims=True)
            moments = jnp.where(slot == axis * len(poly) + term, total, moments)
    moved = moments * (1.0 / slots)
    out[9] = moved
    alone[...] = moved
    for plane, message in ((0, after), (1, before)):
        for index in range(4):
            cell = 2 * index + plane
            message[0:9, index : index + 1, :] = out[0:9, cell : cell + 1, :]
        message[9] = moved[:4]
        message[10] = moved[4:]


def stack_rows(message, pieces, width):
    row = 0
    for piece in pieces:
        count = piece.shape[0]
        layer, start = (9 + row // width, row % width)
        message[layer, start : start + count, :] = piece
        row += count


def pack_x_kernel(own, high, low, *rest):
    middle, message = (rest[:-2], rest[-1])
    message[0:9, 0:8, :] = own[0:9]
    message[0:9, 8:12, :] = high[0:9]
    message[0:9, 12:16, :] = low[0:9]
    pieces = [own[9], high[9], high[10]] + [piece[...] for piece in middle] + [low[9], low[10]]
    stack_rows(message, pieces, 16)


def pack_y_kernel(starts, inner, outer, *rest):
    tails, messages, alone = (rest[: len(starts)], rest[-3:-1], rest[-1])
    for plane, message in enumerate(messages):
        for index, block in enumerate((inner, outer)):
            first = 8 * index
            for half in range(2):
                here, there = (first + 2 * half, 4 * half + 2 * plane)
                message[0:9, here : here + 2, :] = block[0:9, there : there + 2, :]
            for line in range(4):
                here, there = (first + 4 + line, 8 + 2 * line + plane)
                message[0:9, here : here + 1, :] = block[0:9, there : there + 1, :]
        layer = 9
        for start, tail in zip(starts, tails):
            for index in range(start, tail.shape[0]):
                message[layer] = tail[index]
                alone[layer - 9] = tail[index]
                layer += 1


def target_rows(place, line, charge):
    one = jnp.ones_like(place[0])
    rows = []
    for axis in range(3):
        high, middle, low = split(place[axis], 3)
        rows += [high, high, high, middle, middle, low]
    rows += split(dotted(place, place), 3)
    rows += [one, one, one]
    for axis in range(3):
        high, low = split(charge[axis], 2)
        rows += [high, high, low]
    rows += split(dotted(charge, place), 3)
    for first in range(3):
        for second in range(3):
            high, low = split(charge[first] * line[second], 2)
            rows += [high, high, low]
    return rows + [jnp.zeros_like(one)]


def source_rows(place, line, charge):
    one = jnp.ones_like(place[0])
    none = None
    radius, product, own, other = ([], [], [], [])
    for axis in range(3):
        high, middle, low = split(-2.0 * place[axis], 3)
        radius += [high, middle, low, high, middle, high]
        high, middle, low = split(charge[axis], 3)
        own += [high, middle, low, high, middle, high]
    product += [none] * 18
    other += [none] * 18
    radius += [one, one, one]
    own += [none] * 3
    product += [none] * 3
    other += [none] * 3
    radius += split(dotted(place, place) + core_square, 3)
    own += split(-dotted(charge, place), 3)
    product += [none] * 3
    other += [none] * 3
    for axis in range(3):
        high, low = split(-place[axis], 2)
        other += [high, low, high]
    other += [one, one, one]
    radius += [none] * 12
    own += [none] * 12
    product += [none] * 12
    for first in range(3):
        for second in range(3):
            high, low = split(charge[first] * line[second], 2)
            product += [high, low, high]
    product += [none]
    radius += [none] * 28
    own += [none] * 28
    other += [none] * 28
    return [radius, product, own, other]


def moved_block(block, base):
    place = [block[axis] + base[axis] for axis in range(3)]
    return place, [block[3 + axis] for axis in range(3)], [block[6 + axis] for axis in range(3)]


def target_order():
    return [4 * x + 2 * y + z for x in range(2) for z in range(2) for y in range(2)]


def add_targets(block, base, targets, stage):
    for index, row in enumerate(target_rows(*moved_block(block, base))):
        stage[index * cells : (index + 1) * cells, :] = row
    for position, cell in enumerate(target_order()):
        rows = stage[pl.ds(cell, features, stride=cells), :]
        targets[position * slots : (position + 1) * slots, :] = rows.T.astype(bf16)


def add_sources(block, base, columns, parts, positions, stage):
    place, line, charge = moved_block(block, base)
    for form, rows in enumerate(source_rows(place, line, charge)):
        used = [index for index, row in enumerate(rows) if row is not None]
        low, high = (min(used) // 16 * 16, -(-(max(used) + 1) // 16) * 16)
        for index in range(low, high):
            row = jnp.zeros((cells, slots), f32) if rows[index] is None else rows[index]
            stage[index * cells : (index + 1) * cells, :] = row
        for cell in range(cells):
            part = stage[pl.ds(low * cells + cell, high - low, stride=cells), :].astype(bf16)
            first = (positions[cell] * forms + form) * slots
            if low:
                columns[0:low, first : first + slots] = jnp.zeros((low, slots), bf16)
            columns[low:high, first : first + slots] = part
            if high < features:
                rest = jnp.zeros((features - high, slots), bf16)
                columns[high:features, first : first + slots] = rest
    for index, row in enumerate(place + line):
        stage[index * cells : (index + 1) * cells, :] = row
    for cell in range(cells):
        first = positions[cell] * 8
        parts[first : first + 8, :] = stage[pl.ds(cell, 8, stride=cells), :]


def pair_products(mine, columns, first, count):
    width = forms * slots
    start = pl.multiple_of(first * width, width)
    return jnp.dot(mine, columns[:, pl.ds(start, count * width)], preferred_element_type=f32)


def add_pairs(before, after, row, value, parts, first, count):
    start = pl.multiple_of(first * 8, 8)
    sources = []
    for cell in range(count):
        rows = parts[pl.ds(start + cell * 8, 8), :]
        sources.append([jnp.broadcast_to(rows[i : i + 1], (8, slots)) for i in range(6)])
    for group in range(value.shape[0] // 8):
        here = slice(group * 8, group * 8 + 8)
        sums = [None] * 4
        for cell in range(count):
            radius, product, own, other = (
                value[here, (cell * forms + form) * slots : (cell * forms + form + 1) * slots]
                for form in range(forms)
            )
            inverse = lax.rsqrt(radius)
            square = inverse * inverse
            cube = inverse * square
            along = product * cube
            across = (own * other) * (square * cube)
            terms = [along * sources[cell][a] + across * sources[cell][3 + a] for a in range(3)]
            terms.append(along)
            sums = [term if s is None else s + term for s, term in zip(sums, terms)]
        for index in range(4):
            place = pl.ds(pl.multiple_of(row + index * cells * slots + group * 8, 8), 8)
            after[place, :] = sums[index] if before is None else before[place, :] + sums[index]


def own_cells():
    return [(x + 1, y + 1, z + 1) for x in range(2) for y in range(2) for z in range(2)]


def z_cells():
    return [(x + 1, y + 1, z) for z in (3, 0) for x in range(2) for y in range(2)]


def x_cells():
    near = [(x, y + 1, z + 1) for x in (3, 0) for y in range(2) for z in range(2)]
    return [near, [(x, y + 1, z) for z in (3, 0) for x in (3, 0) for y in range(2)]]


def y_cells(y):
    result = []
    for xs in ((1, 2), (3, 0)):
        cell = [(x, y, z + 1) for x in xs for z in range(2)]
        result.append(cell + [(x, y, z) for z in (3, 0) for x in xs])
    return result


def base_of(places):
    row = lax.broadcasted_iota(jnp.int32, (cells, slots), 0)
    result = []
    for axis in range(3):
        value = jnp.full((cells, slots), places[0][axis] - 1.5, f32)
        for cell in range(1, cells):
            if places[cell][axis] != places[0][axis]:
                value = jnp.where(row == cell, places[cell][axis] - 1.5, value)
        result.append(value)
    return result


def near_sums(
    targets, groups, tasks_of, before, after, columns, parts, stage, unroll=2, finish=None
):
    for block, places, positions in groups:
        add_sources(block, base_of(places), columns, parts, positions, stage)

    def several_pairs(step, carry):
        tasks = []
        for index in range(unroll):
            pair = step * unroll + index
            tasks += [(index, pair, task) for task in tasks_of(pair // 2, pair % 2)]

        def products(index, pair, task):
            row = pl.multiple_of((pair * 2 + task[0]) * slots, slots)
            mine = targets[pl.ds(row, task[1] * slots), :]
            return row, pair_products(mine, columns, *task[2:])

        ready = products(*tasks[0])
        seen = None
        for order, (index, pair, task) in enumerate(tasks):
            following = tasks[order + 1] if order + 1 < len(tasks) else None
            later = products(*following) if following else None
            now = (index, task[0])
            add_pairs(after if now == seen else before, after, *ready, parts, *task[2:])
            seen = now
            if finish and (following is None or (following[0], following[2][0]) != now):
                finish(pair * 2 + task[0], pair // 2 * 4 + pair % 2 + 2 * task[0])
            ready = later
        return carry

    lax.fori_loop(0, cells // 2 // unroll, several_pairs, 0)


def rows_of(block, first=0):
    return [block[axis, first : first + cells, :] for axis in range(9)]


def own_kernel(own, message, targets, sums, *scratch):
    add_targets(rows_of(own), base_of(own_cells()), targets, scratch[2])
    groups = [(rows_of(own), own_cells(), list(range(8)))]

    def tasks(x, z):
        return [(0, 2, first, 2) for first in (0, 2, 4, 6)]

    near_sums(targets, groups, tasks, None, sums, *scratch)


def z_kernel(targets, halo, before, after, *scratch):
    groups = [(rows_of(halo, 8), z_cells(), list(range(8)))]

    def tasks(x, z):
        return [(0, 2, 4 * (1 - z) + first, 2) for first in (0, 2)]

    near_sums(targets, groups, tasks, before, after, *scratch, unroll=4)


def x_kernel(targets, halo, message, before, after, *scratch):
    groups = []
    for index, places in enumerate(x_cells()):
        positions = [(0 if x == 3 else 8) + 2 * z + y - 1 for x, y, z in places]
        groups.append((rows_of(halo, 8 * index), places, positions))

    def tasks(x, z):
        return [(0, 2, 8 * (1 - x) + 2 * z + first, 2) for first in (0, 2, 4)]

    near_sums(targets, groups, tasks, before, after, *scratch)


def y_kernel(
    starts, stress, mobility, counts, own, targets, high, low, before, weights_far, translation, *rest
):
    tails, out, scratch = (rest[: len(starts)], rest[len(starts)], rest[len(starts) + 1 :])
    after, gathered = scratch[-2:]
    groups = []
    for block, side in ((high, 3), (low, 0)):
        for index, places in enumerate(y_cells(side)):
            positions = [(16 if side else 0) + 4 * x + z for x, y, z in places]
            groups.append((rows_of(block, 8 * index), places, positions))

    def tasks(x, z):
        return [(y, 1, 16 * y + 4 * (x + line) + z, 3) for y in range(2) for line in range(3)]

    local = [tail[index] for start, tail in zip(starts, tails) for index in range(start, tail.shape[0])]
    coefficients = jnp.dot(
        weights_far[...],
        jnp.concatenate(local, axis=0),
        precision=highest,
        preferred_element_type=f32,
    )
    coefficients = jnp.dot(
        coefficients, translation[...], precision=highest, preferred_element_type=f32
    )
    place = [own[axis] for axis in range(3)]
    line = [own[3 + axis] for axis in range(3)]
    charge = [own[6 + axis] for axis in range(3)]
    base = base_of(own_cells())
    poly = monomials(place)
    mask = (lax.broadcasted_iota(jnp.int32, (cells, slots), 1) < by_cell(counts)).astype(f32)
    stressed = [
        stress[a, 0] * charge[0] + stress[a, 1] * charge[1] + stress[a, 2] * charge[2]
        for a in range(3)
    ]
    applied = crossed(stressed, line)
    outside = []
    for axis in range(3):
        far = jnp.zeros((cells, slots), f32)
        for term, value in enumerate(poly):
            column = axis * len(poly) + term
            coefficient = coefficients[:, column : column + 1]
            far = far + (coefficient if value is None else coefficient * value)
        outside.append(far * mask + applied[axis])
    scale = by_cell(mobility) * mask
    lane = lax.broadcasted_iota(jnp.int32, (slots, slots), 1)

    def finish(position, cell):
        for index in range(4):
            first = pl.multiple_of((index * cells + position) * slots, slots)
            total = jnp.sum(after[pl.ds(first, slots), :], axis=1, keepdims=True)
            gathered[...] = jnp.where(lane == index * cells + cell, total, gathered[...])

    gathered[...] = jnp.zeros((slots, slots), f32)
    near_sums(targets, groups, tasks, before, after, *scratch[:-2], finish=finish)
    mixed = gathered[...].T
    sums_of = [mixed[index * cells : (index + 1) * cells, :] for index in range(4)]
    force = []
    for axis in range(3):
        at = place[axis] + base[axis]
        near = sums_of[axis] - at * sums_of[3]
        force.append(near_scale * near + outside[axis])
    ratio = dotted(force, line) / jnp.maximum(dotted(line, line), 1.0)
    for axis in range(3):
        out[axis] = scale * (force[axis] - ratio * line[axis])


def far_weights(sizes):
    corners = list(itertools.product(range(2), repeat=3))
    result = []
    for here in corners:
        line = []
        for y, x, z in itertools.product(range(sizes[1]), range(sizes[0]), range(sizes[2])):
            for there in corners:
                gaps = []
                for axis, step in enumerate((x, y, z)):
                    extent = 2 * sizes[axis]
                    gap = (2 * step + there[axis] - here[axis]) % extent
                    gaps.append(min(gap, extent - gap))
                apart = math.sqrt(sum(gap * gap for gap in gaps))
                line.append(1.0 / apart if max(gaps) > 1 else 0.0)
        result.append(line)
    return np.asarray(result, np.float32)


def shifted(value, axis, step):
    count = lax.axis_size(axis)
    return lax.ppermute(value, axis, [(i, (i - step) % count) for i in range(count)])


def near_call(kernel, name, count, pairs, scalars, arrays, shape, last=False):
    vmem = pl.BlockSpec(memory_space=pltpu.VMEM)
    smem = pl.BlockSpec(memory_space=pltpu.SMEM)
    scratch = [
        pltpu.VMEM((features, count * forms * slots), bf16),
        pltpu.VMEM((count * 8, slots), f32),
        pltpu.VMEM((features * cells, slots), f32),
    ]
    if last:
        scratch.append(pltpu.VMEM((4 * cells * slots, slots), f32))
        scratch.append(pltpu.VMEM((slots, slots), f32))
    return pl.pallas_call(
        kernel,
        out_shape=shape,
        in_specs=[smem] * len(scalars) + [vmem] * len(arrays),
        out_specs=jax.tree.map(lambda leaf: vmem, shape),
        scratch_shapes=scratch,
        compiler_params=pltpu.CompilerParams(vmem_limit_bytes=8 * 1024 * 1024),
        cost_estimate=pl.CostEstimate(
            flops=pairs * slots * slots * 8000, bytes_accessed=1 << 20, transcendentals=0
        ),
        name=name,
    )(*scalars, *arrays)


def body(offsets, lines, burgers, counts, mobility, stress, translation):
    sizes = [lax.axis_size(axis) for axis in ("gx", "gy", "gz")]
    segments = jnp.concatenate([offsets, lines, burgers], axis=0).reshape(9, cells, slots)
    vmem = pl.BlockSpec(memory_space=pltpu.VMEM)
    smem = pl.BlockSpec(memory_space=pltpu.SMEM)
    message = jax.ShapeDtypeStruct((11, 4, slots), f32)
    block = jax.ShapeDtypeStruct((10, cells, slots), f32)
    own, up, down, moments = pl.pallas_call(
        prepare_kernel,
        out_shape=(block, message, message, jax.ShapeDtypeStruct((cells, slots), f32)),
        in_specs=[smem, vmem],
        out_specs=(vmem,) * 4,
        compiler_params=pltpu.CompilerParams(vmem_limit_bytes=4 * 1024 * 1024),
        name="prepare",
    )(counts, segments)
    high = shifted(up, "gz", 1)
    low = shifted(down, "gz", -1)
    middle = [shifted(moments, "gz", step) for step in range(2, sizes[2] - 1)]
    sums = jax.ShapeDtypeStruct((4 * cells * slots, slots), f32)
    both = (jax.ShapeDtypeStruct((cells * slots, features), bf16), sums)
    targets, partial = near_call(own_kernel, "near_own", 8, 64, [], [own, up], both)
    message = pl.pallas_call(
        pack_x_kernel,
        out_shape=jax.ShapeDtypeStruct((9 + sizes[2] // 2, 16, slots), f32),
        in_specs=[vmem] * (4 + len(middle)),
        out_specs=vmem,
        compiler_params=pltpu.CompilerParams(vmem_limit_bytes=4 * 1024 * 1024),
        name="pack_x",
    )(own, high, low, *middle, partial)
    if sizes[0] == 2:
        outer = shifted(message, "gx", 1)
        starts, tails = ([9, 9], [message, outer])
    else:
        moments = message[9:].reshape(-1, slots)
        tail = moments.reshape(-1, 8, slots)
        planes = []
        for plane in (0, 1):
            part = [
                message[:9, :8].reshape(9, 2, 4, slots)[:, plane],
                message[:9, 8:].reshape(9, 2, 2, 2, slots)[:, :, plane].reshape(9, 4, slots),
            ]
            planes.append(jnp.concatenate([jnp.concatenate(part, axis=1), tail], axis=0))
        after = shifted(planes[0], "gx", 1)
        before = shifted(planes[1], "gx", -1)
        others = [shifted(moments, "gx", step) for step in range(2, sizes[0] - 1)]
        both = [after[:9], before[:9]]
        sides = [value[:, 4:].reshape(9, 2, 1, 2, slots) for value in both]
        sides = jnp.concatenate(sides, axis=2).reshape(9, 8, slots)
        outer = jnp.concatenate([value[:, :4] for value in both] + [sides], axis=1)
        moments = jnp.concatenate(
            [moments, after[9:].reshape(-1, slots)] + others + [before[9:].reshape(-1, slots)],
            axis=0,
        )
        starts, tails = ([0], [moments.reshape(-1, 16, slots)])
    partial = near_call(z_kernel, "near_z", 8, 32, [], [targets, message, partial], sums)
    layers = 9 + sum(tail.shape[0] - start for start, tail in zip(starts, tails))
    face = jax.ShapeDtypeStruct((layers, 16, slots), f32)
    up, down, moments = pl.pallas_call(
        functools.partial(pack_y_kernel, starts),
        out_shape=(face, face, jax.ShapeDtypeStruct((layers - 9, 16, slots), f32)),
        in_specs=[vmem] * (3 + len(tails)),
        out_specs=(vmem,) * 3,
        compiler_params=pltpu.CompilerParams(vmem_limit_bytes=4 * 1024 * 1024),
        name="pack_y",
    )(message, outer, *tails, partial)
    high = shifted(up, "gy", 1)
    low = shifted(down, "gy", -1)
    middle = [shifted(moments, "gy", step) for step in range(2, sizes[1] - 1)]
    partial = near_call(x_kernel, "near_x", 16, 48, [], [targets, outer, up, partial], sums)
    starts = starts + [9] + [0] * len(middle) + [9]
    tails = tails + [high] + middle + [low]
    out = near_call(
        functools.partial(y_kernel, starts),
        "near_y",
        32,
        72,
        [stress, mobility, counts],
        [own, targets, high, low, partial, jnp.asarray(far_weights(sizes)), translation] + tails,
        jax.ShapeDtypeStruct((3, cells, slots), f32),
        last=True,
    )
    return out.reshape(3, 2, 2, 2, slots)


def solution(mesh):
    placed = (
        P(None, "gx", "gy", "gz", None),
        P(None, "gx", "gy", "gz", None),
        P(None, "gx", "gy", "gz", None),
        P("gx", "gy", "gz"),
        P("gx", "gy", "gz"),
        P(),
        P(),
    )
    return jax.shard_map(
        body, mesh=mesh, in_specs=placed, out_specs=P(None, "gx", "gy", "gz", None), check_vma=False
    )
```
